768 devices in a mesh: dp: 4 (over x), ctx: 32 (over z_hi, y), mp: 6 (over z_lo, core).
Axes of the slice: x: 4, y: 8, z: 12 (z_hi: 4, z_lo: 3; z = z_hi * 3 + z_lo), core: 2. Of those that a mesh axis runs over, the one named last changes fastest.
Arguments:
- streams: bfloat16 [16384, 3, 4608], P(('dp', 'ctx'), None, 'mp'), parts along dimension 0, may hold values from -6 to 6
- short_taps: float32 [7, 3, 288], P(None, None, 'mp'), may hold values from -2.5 to 2.5
- modal_residue: float32 [16, 288], P(None, 'mp'), may hold values from -0.09 to 0.09
- modal_rate: float32 [16, 288], P(None, 'mp'), may hold values from 1.2207031e-05 to 0.03
- skip_gain: float32 [4608], P('mp'), may hold values from -4 to 4
- queries: bfloat16 [16384, 48, 128], P(('dp', 'ctx'), 'mp'), parts along dimension 0, may hold values from -9 to 9
- keys: bfloat16 [16384, 6, 128], P(('dp', 'ctx'), 'mp'), parts along dimension 0, may hold values from -9 to 9
- values: bfloat16 [16384, 6, 128], P(('dp', 'ctx'), 'mp'), parts along dimension 0, may hold values from -6 to 6
Outputs:
- hyena_out: bfloat16 [16384, 4608], P(('dp', 'ctx'), 'mp'), parts along dimension 0
- attn_out: bfloat16 [16384, 48, 128], P(('dp', 'ctx'), 'mp'), parts along dimension 0
The draws below stay inside these ranges and needn't reach their ends.
There are 4 independent parts, one for each index of `dp`. The reference program is written for one: setup_inputs(seed, part) draws one part's arguments, and reference() takes and returns one part's arrays. A program takes and returns all parts, laid end to end along the dimension named above; an argument that names none is the same for every part. Nothing has to cross between parts.
All inputs are finite; a program needn't handle non-finite values.
Results may differ from the reference program's by a relative error of at most 0.01.
Values may be sent and summed in bfloat16 or wider, within the bound.
No kernel may reach another device: no remote copies, remote signals or barrier semaphores. Data moves between devices by JAX's collectives and lax.ppermute only.
A program may use at most 64 MiB of HBM per device.

```python
import math
import jax
import jax.numpy as jnp
from jax import lax

GSIZE = 16
TAPS = 7
MODES = 16
HD = 128
GROUP = 8
LEN = 4096
CHANNELS = 4608
GROUPS = 288
HEADS = 48
KV_HEADS = 6


def query_key_pair(key):
    parts = jax.random.split(jax.random.fold_in(key, 7), 2)
    query_draw = jnp.clip(3.0 * jax.random.normal(parts[0], (LEN, HEADS, HD), jnp.float32), -9.0, 9.0)
    key_draw = jnp.clip(jax.random.normal(parts[1], (LEN, KV_HEADS, HD), jnp.float32), -6.0, 6.0)
    return (query_draw, key_draw)


def draw_queries(key, part):
    return query_key_pair(key)[0].astype(jnp.bfloat16)


def draw_keys(key, part):
    return query_key_pair(key)[1].astype(jnp.bfloat16)


def steps_of(key, extent, cuts, low, high):
    loudness, own = 1.0, jax.random.fold_in(key, 6)
    for dim, blocks in cuts:
        heights = jnp.exp(jax.random.uniform(jax.random.fold_in(own, dim), (blocks,), jnp.float32, low / len(cuts), high / len(cuts)))
        loudness = loudness * jnp.repeat(heights, extent[dim] // blocks).reshape([-1 if axis == dim else 1 for axis in range(len(extent))])
    return loudness


def bell_draw(stream_key, dims, deviation, limit, shards=(), held_as=jnp.bfloat16):
    drawn = jax.random.normal(stream_key, dims, jnp.float32) * deviation
    if len(shards) > 0:
        drawn = steps_of(stream_key, dims, shards, -0.22, 0.18) * drawn
    return jnp.clip(drawn, min=-limit, max=limit).astype(held_as)


def setup_inputs(seed: int = 0, part: int = 0) -> dict:
    streams_of = jax.random.split(jax.random.key(seed), 9)
    own_keys = jax.random.split(jax.random.fold_in(streams_of[8], part), 9)
    streams = bell_draw(own_keys[0], (LEN, 3, CHANNELS), 1.0, 6.0, ((0, 32), (2, 6)))
    short_taps = bell_draw(streams_of[1], (TAPS, 3, GROUPS), 0.3, 2.5, ((2, 6),), jnp.float32)
    modal_residue = bell_draw(streams_of[2], (MODES, GROUPS), 0.015, 0.09, ((1, 6),), jnp.float32)
    modal_rate = jnp.clip(jnp.exp(math.log(0.03) - 7.8069405 * jax.random.uniform(streams_of[3], (MODES, GROUPS), jnp.float32) ** steps_of(streams_of[3], (MODES, GROUPS), ((1, 6),), -0.2, 0.2)), 1.220703143189894e-05, 0.03)
    skip_gain = bell_draw(streams_of[4], (CHANNELS,), 1.0, 4.0, ((0, 6),), jnp.float32)
    queries = draw_queries(jax.random.fold_in(jax.random.fold_in(streams_of[8], part), 71), part)
    keys = draw_keys(jax.random.fold_in(jax.random.fold_in(streams_of[8], part), 71), part)
    values = bell_draw(own_keys[7], (LEN, KV_HEADS, HD), 1.0, 6.0, ((0, 32), (1, 6)))
    return dict(streams=streams, short_taps=short_taps, modal_residue=modal_residue, modal_rate=modal_rate, skip_gain=skip_gain, queries=queries, keys=keys, values=values)


def short_filter(streams, short_taps):
    taps_full = jnp.repeat(short_taps, GSIZE, axis=2)
    padded = jnp.pad(streams.astype(jnp.float32), ((TAPS - 1, 0), (0, 0), (0, 0)))
    filtered = jnp.zeros(streams.shape, jnp.float32)
    for offset in range(TAPS):
        filtered = filtered + taps_full[offset] * padded[TAPS - 1 - offset:TAPS - 1 - offset + LEN]
    return filtered

def attend_head(operands):
    query_head, key_head, value_head = operands
    block = min(512, LEN)
    count = LEN // block
    scale = 1.0 / math.sqrt(HD)
    positions = jnp.arange(LEN, dtype=jnp.int32)
    key_float = key_head.astype(jnp.float32)
    value_float = value_head.astype(jnp.float32)
    query_blocks = query_head.reshape(count, block, GROUP, HD)

    def one_block(item):
        query_block, number = item
        scores = jnp.einsum('thd,sd->hts', query_block.astype(jnp.float32), key_float) * scale
        target = number * block + jnp.arange(block, dtype=jnp.int32)
        visible = positions[None, None, :] <= target[None, :, None]
        masked = jnp.where(visible, scores, -1e+30)
        largest = lax.optimization_barrier(jnp.max(masked, axis=-1, keepdims=True))
        weights = jnp.where(visible, jnp.exp(scores - largest), 0.0)
        total = lax.optimization_barrier(jnp.sum(weights, axis=-1))
        rounded = lax.optimization_barrier(weights.astype(jnp.bfloat16))
        mixed = jnp.einsum('hts,sd->htd', rounded.astype(jnp.float32), value_float)
        return (mixed / total[..., None]).astype(jnp.bfloat16)
    result = lax.map(one_block, (query_blocks, jnp.arange(count, dtype=jnp.int32)))
    return jnp.transpose(result, (0, 2, 1, 3)).reshape(LEN, GROUP, HD)

def reference(streams, short_taps, modal_residue, modal_rate, skip_gain, queries, keys, values):
    filtered = short_filter(streams, short_taps)
    gated = (filtered[:, 1] * filtered[:, 2]).astype(jnp.bfloat16)
    lags = jnp.arange(LEN, dtype=jnp.float32)
    table = lax.optimization_barrier(jnp.sum(modal_residue[:, None, :] * jnp.exp(-modal_rate[:, None, :] * lags[None, :, None]), axis=0))
    table_full = jnp.repeat(table, GSIZE, axis=1)
    length = 2 * LEN
    spectrum = jnp.fft.rfft(gated.astype(jnp.float32), n=length, axis=0) * jnp.fft.rfft(table_full, n=length, axis=0)
    long_term = jnp.fft.irfft(spectrum, n=length, axis=0)[:LEN]
    hyena_out = (filtered[:, 0] * (long_term + skip_gain * gated.astype(jnp.float32))).astype(jnp.bfloat16)
    query_heads = jnp.transpose(queries.reshape(LEN, KV_HEADS, GROUP, HD), (1, 0, 2, 3))
    key_heads = jnp.transpose(keys, (1, 0, 2))
    value_heads = jnp.transpose(values, (1, 0, 2))
    mixed = lax.map(attend_head, (query_heads, key_heads, value_heads))
    attn_out = jnp.transpose(mixed, (1, 0, 2, 3)).reshape(LEN, HEADS, HD)
    return (hyena_out, attn_out)
```

```python
import functools
import math

import jax
import jax.numpy as jnp
from jax import lax
from jax.experimental import pallas as pl
from jax.experimental.pallas import tpu as pltpu
from jax.sharding import Mesh, PartitionSpec as P

GSIZE = 16
LANES = 128
LOG2E = 1.4426950408889634
HIGHEST = lax.Precision.HIGHEST
F32 = jnp.float32
BF16 = jnp.bfloat16


def vmem(count):
    return [pl.BlockSpec(memory_space=pltpu.VMEM)] * count


def smem():
    return pl.BlockSpec(memory_space=pltpu.SMEM)


def call(kernel, out_shape, in_specs, flops, moved, scratch=()):
    many = isinstance(out_shape, (list, tuple))
    return pl.pallas_call(
        kernel,
        out_shape=out_shape,
        in_specs=in_specs,
        out_specs=vmem(len(out_shape)) if many else vmem(1)[0],
        scratch_shapes=list(scratch),
        compiler_params=pltpu.CompilerParams(vmem_limit_bytes=32 * 1024 * 1024),
        cost_estimate=pl.CostEstimate(flops=flops, bytes_accessed=moved, transcendentals=0),
    )


def iota(shape, dim):
    return lax.broadcasted_iota(jnp.int32, shape, dim)


def split(value):
    high = value.astype(BF16)
    return high, (value - high.astype(F32)).astype(BF16)


def filter_kernel(st_ref, rim_ref, taps_ref, rate_ref, first_ref, gated_ref, state_ref, ext):
    rows, width = gated_ref.shape
    pad = rim_ref.shape[1]
    taps = taps_ref.shape[0] // 3
    row = iota((rows, LANES), 0).astype(F32)
    same = iota((LANES, LANES), 0) // GSIZE == iota((LANES, LANES), 1) // GSIZE
    for tile in range(width // LANES):
        cols = slice(tile * LANES, (tile + 1) * LANES)
        for j in range(3):
            ext[j, :pad, :] = rim_ref[j, :, cols].astype(F32)
            ext[j, pad:, :] = st_ref[j, :, cols].astype(F32)
        filtered = []
        for j in range(3):
            total = taps_ref[j : j + 1, cols] * ext[j, pad : pad + rows, :]
            for k in range(1, taps):
                tap = taps_ref[3 * k + j : 3 * k + j + 1, cols]
                total = total + tap * ext[j, pad - k : pad - k + rows, :]
            filtered.append(total)
        first_ref[:, cols] = filtered[0]
        gated = (filtered[1] * filtered[2]).astype(BF16)
        gated_ref[:, cols] = gated
        decay = jnp.exp(-rate_ref[:, cols] * (float(rows) - row)).T
        high, low = split(decay)
        full = jnp.dot(high, gated, preferred_element_type=F32) + jnp.dot(
            low, gated, preferred_element_type=F32
        )
        full = jnp.where(same, full, 0.0)
        state = full[:GSIZE]
        for g in range(1, LANES // GSIZE):
            state = state + full[g * GSIZE : (g + 1) * GSIZE]
        state_ref[:, cols] = state


def near_kernel(gated_ref, rate_ref, res_ref, near_ref):
    rows, width = gated_ref.shape
    per = LANES // GSIZE
    row = iota((rows, LANES), 0).astype(F32)
    group = iota((rows, LANES), 1) // GSIZE
    causal = iota((rows, LANES), 0) >= iota((rows, LANES), 1)
    for tile in range(width // LANES):
        cols = slice(tile * LANES, (tile + 1) * LANES)
        rate = rate_ref[:, cols]
        coeff = res_ref[:, cols] * jnp.exp(-rate * row)
        grow = jnp.exp(rate * row).T
        gated = gated_ref[:, cols]
        grow_high, grow_low = split(grow)
        coeff_high, coeff_low = split(coeff)
        zero = jnp.zeros_like(coeff_high)
        stack_high = jnp.concatenate([jnp.where(group == g, coeff_high, zero) for g in range(per)], 0)
        stack_low = jnp.concatenate([jnp.where(group == g, coeff_low, zero) for g in range(per)], 0)
        table = (
            jnp.dot(stack_high, grow_high, preferred_element_type=F32)
            + jnp.dot(stack_high, grow_low, preferred_element_type=F32)
            + jnp.dot(stack_low, grow_high, preferred_element_type=F32)
        )
        table = jnp.where(jnp.concatenate([causal] * per, 0), table, 0.0).astype(BF16)
        every = jnp.dot(table, gated, preferred_element_type=F32)
        near = jnp.zeros((rows, LANES), F32)
        for g in range(per):
            near = jnp.where(group == g, every[g * rows : (g + 1) * rows], near)
        near_ref[:, cols] = near


def join_kernel(first_ref, gated_ref, near_ref, past_ref, rate_ref, res_ref, gain_ref, out_ref):
    rows, width = gated_ref.shape
    row = iota((rows, LANES), 0).astype(F32)
    same = iota((LANES, LANES), 0) // GSIZE == iota((LANES, LANES), 1) // GSIZE
    for tile in range(width // LANES):
        cols = slice(tile * LANES, (tile + 1) * LANES)
        coeff_high, coeff_low = split(res_ref[:, cols] * jnp.exp(-rate_ref[:, cols] * row))
        past = jnp.concatenate([past_ref[:, cols]] * (LANES // GSIZE), 0)
        past_high, past_low = split(jnp.where(same, past, 0.0))
        far = (
            jnp.dot(coeff_high, past_high, preferred_element_type=F32)
            + jnp.dot(coeff_high, past_low, preferred_element_type=F32)
            + jnp.dot(coeff_low, past_high, preferred_element_type=F32)
        )
        direct = gain_ref[:, cols] * gated_ref[:, cols].astype(F32)
        out_ref[:, cols] = (first_ref[:, cols] * (far + near_ref[:, cols] + direct)).astype(BF16)


def attend_kernel(first, last, rows, scale, where_ref, q_ref, kv_ref, *refs):
    blocks = kv_ref.shape[0] // rows
    heads = q_ref.shape[0] // rows
    if first:
        acc_out, ml_out = refs
    elif last:
        acc_in, ml_in, out_ref = refs
    else:
        acc_in, ml_in, acc_out, ml_out = refs
    chunk = 256
    keys = kv_ref[:, :LANES]
    values = jnp.concatenate([kv_ref[:, LANES:], jnp.ones((kv_ref.shape[0], LANES), BF16)], 1)
    lane_block = iota((1, kv_ref.shape[0]), 1) // rows
    bias = jnp.zeros((1, kv_ref.shape[0]), F32)
    for b in range(1 if first else 0, blocks):
        bias = bias + jnp.where((lane_block == b) & (where_ref[b] == 0), -1e30, 0.0)

    for number in range(q_ref.shape[0] // chunk):
        span = slice(number * chunk, (number + 1) * chunk)
        scores = lax.dot_general(
            q_ref[span, :], keys, (((1,), (1,)), ((), ())), preferred_element_type=F32
        )
        scores = scores * scale + bias
        if first:
            target = (number * chunk + iota(scores.shape, 0)) // heads
            source = iota(scores.shape, 1)
            scores = jnp.where((source > target) & (source < rows), -1e30, scores)
        largest = jnp.max(scores, axis=1, keepdims=True)
        if not first:
            before = ml_in[span, :1]
            largest = jnp.maximum(largest, before)
        weights = jnp.exp2(scores - largest).astype(BF16)
        mixed = jnp.dot(weights, values, preferred_element_type=F32)
        total = mixed[:, LANES : 2 * LANES]
        mixed = mixed[:, :LANES]
        if not first:
            shrink = jnp.exp2(before - largest)
            mixed = mixed + acc_in[span, :] * shrink
            total = total + ml_in[span, LANES - 1 :] * shrink
        if last:
            out_ref[span, :] = (mixed / total).astype(BF16)
        else:
            acc_out[span, :] = mixed
            lane = iota((chunk, LANES), 1)
            ml_out[span, :] = jnp.where(lane < LANES // 2, largest, total)


def body(streams, short_taps, modal_residue, modal_rate, skip_gain, queries, keys, values):
    rows, kinds, width = streams.shape
    taps = short_taps.shape[0]
    modes, groups = modal_rate.shape
    heads, size = queries.shape[1:]
    layers, ring, parts = lax.axis_size("zh"), lax.axis_size("y"), lax.axis_size("mp")
    layer, place = lax.axis_index("zh"), lax.axis_index("y")
    side = lax.axis_index("mp") % 2
    devices = layers * ring

    kv = jnp.concatenate([keys[:, 0], values[:, 0]], axis=1)
    held = [kv] + [
        lax.ppermute(kv, "zh", [(z, z + s) for z in range(layers - s)]) for s in range(1, layers)
    ]
    held = jnp.concatenate(held, axis=0)

    by_kind = jnp.transpose(streams, (1, 0, 2))
    rim = lax.ppermute(by_kind[:, rows - 8 :], ("zh", "y"), [(i, i + 1) for i in range(devices - 1)])
    taps_full = jnp.repeat(short_taps.reshape(taps * kinds, groups), GSIZE, axis=1)
    rate_full = jnp.repeat(modal_rate, GSIZE, axis=1)
    rate_row = modal_rate.T.reshape(1, groups * modes)
    res_row = modal_residue.T.reshape(1, groups * modes)
    wide = jax.ShapeDtypeStruct((rows, width), F32)
    first, gated, state = call(
        filter_kernel,
        [wide, jax.ShapeDtypeStruct((rows, width), BF16), jax.ShapeDtypeStruct((modes, width), F32)],
        vmem(4),
        4_000_000_000,
        4_000_000,
        [pltpu.VMEM((3, rows + 8, LANES), F32)],
    )(by_kind, rim, taps_full, rate_row)
    near = call(near_kernel, wide, vmem(3), 4_000_000_000, 4_000_000)(gated, rate_row, res_row)

    past = jnp.zeros_like(state)
    step_rate = -rate_full * float(rows)
    step = 1
    while step < devices:
        full = state + jnp.exp(step_rate) * past
        come = lax.ppermute(full, ("zh", "y"), [(i, i + step) for i in range(devices - step)])
        past = past + jnp.exp(step_rate * (step - 1.0)) * come
        step *= 2
    hyena_out = call(
        join_kernel,
        jax.ShapeDtypeStruct((rows, width), BF16),
        vmem(7),
        500_000_000,
        2_000_000,
    )(first, gated, near, past, rate_row, res_row, skip_gain.reshape(1, width))

    rows_q = queries.reshape(rows * heads, size)
    scale = LOG2E / math.sqrt(size)
    pairs = [
        (y * parts + m, ((y + (1 if m % 2 == 0 else -1)) % ring) * parts + m)
        for y in range(ring)
        for m in range(parts)
    ]
    state_shape = [jax.ShapeDtypeStruct((rows * heads, LANES), F32)] * 2
    carry = ()
    attn_out = None
    for step in range(ring):
        origin = (place + jnp.where(side == 0, -step, step)) % ring
        visible = jnp.concatenate(
            [(origin < place)[None], layer >= jnp.arange(1, layers)]
        ).astype(jnp.int32)
        last = step == ring - 1
        carry = call(
            functools.partial(attend_kernel, step == 0, last, rows, scale),
            jax.ShapeDtypeStruct((rows * heads, size), BF16) if last else state_shape,
            [smem()] + vmem(2 + len(carry)),
            1_000_000_000,
            3_000_000,
        )(visible, rows_q, held, *carry)
        if not last:
            held = lax.ppermute(held, ("y", "mp"), pairs)
    attn_out = carry.reshape(rows, heads, size)
    return hyena_out, attn_out


def solution(mesh):
    names = ("dp", "zh", "y", "mp")
    dp, ctx, mp = (mesh.shape[name] for name in ("dp", "ctx", "mp"))
    ring = 8 if ctx % 8 == 0 else ctx
    finer = Mesh(mesh.devices.reshape(dp, ctx // ring, ring, mp), names)
    pos = ("dp", "zh", "y")
    in_specs = (
        P(pos, None, "mp"),
        P(None, None, "mp"),
        P(None, "mp"),
        P(None, "mp"),
        P("mp"),
        P(pos, "mp", None),
        P(pos, "mp", None),
        P(pos, "mp", None),
    )
    out_specs = (P(pos, "mp"), P(pos, "mp", None))
    return jax.shard_map(body, mesh=finer, in_specs=in_specs, out_specs=out_specs, check_vma=False)
```

```python
import functools
import math

import jax
import jax.numpy as jnp
from jax import lax
from jax.experimental import pallas as pl
from jax.experimental.pallas import tpu as pltpu
from jax.sharding import Mesh, PartitionSpec as P

GSIZE = 16
LANES = 128
LOG2E = 1.4426950408889634
HIGHEST = lax.Precision.HIGHEST
F32 = jnp.float32
BF16 = jnp.bfloat16


def vmem(count):
    return [pl.BlockSpec(memory_space=pltpu.VMEM)] * count


def smem():
    return pl.BlockSpec(memory_space=pltpu.SMEM)


def call(kernel, out_shape, in_specs, flops, moved, scratch=()):
    many = isinstance(out_shape, (list, tuple))
    return pl.pallas_call(
        kernel,
        out_shape=out_shape,
        in_specs=in_specs,
        out_specs=vmem(len(out_shape)) if many else vmem(1)[0],
        scratch_shapes=list(scratch),
        compiler_params=pltpu.CompilerParams(vmem_limit_bytes=32 * 1024 * 1024),
        cost_estimate=pl.CostEstimate(flops=flops, bytes_accessed=moved, transcendentals=0),
    )


def iota(shape, dim):
    return lax.broadcasted_iota(jnp.int32, shape, dim)


def split(value):
    high = value.astype(BF16)
    return high, (value - high.astype(F32)).astype(BF16)


def filter_kernel(st_ref, rim_ref, taps_ref, rate_ref, first_ref, gated_ref, state_ref, ext):
    rows, width = gated_ref.shape
    pad = rim_ref.shape[1]
    taps = taps_ref.shape[0] // 3
    modes = LANES // (LANES // GSIZE)
    row = iota((rows, LANES), 0).astype(F32)
    same = iota((LANES, LANES), 0) // GSIZE == iota((LANES, LANES), 1) // GSIZE
    for tile in range(width // LANES):
        cols = slice(tile * LANES, (tile + 1) * LANES)
        for j in range(3):
            ext[j, :pad, :] = rim_ref[j, :, cols].astype(F32)
            ext[j, pad:, :] = st_ref[j, :, cols].astype(F32)
        filtered = []
        for j in range(3):
            total = taps_ref[j : j + 1, cols] * ext[j, pad : pad + rows, :]
            for k in range(1, taps):
                tap = taps_ref[3 * k + j : 3 * k + j + 1, cols]
                total = total + tap * ext[j, pad - k : pad - k + rows, :]
            filtered.append(total)
        first_ref[:, cols] = filtered[0]
        gated = (filtered[1] * filtered[2]).astype(BF16)
        gated_ref[:, cols] = gated
        decay = jnp.exp(-rate_ref[:, cols] * (float(rows) - row)).T
        high, low = split(decay)
        full = jnp.dot(high, gated, preferred_element_type=F32) + jnp.dot(
            low, gated, preferred_element_type=F32
        )
        full = jnp.where(same, full, 0.0)
        state = full[:modes]
        for g in range(1, LANES // GSIZE):
            state = state + full[g * modes : (g + 1) * modes]
        high, low = split(state)
        band, half = tile // 2, slice(tile % 2 * LANES, (tile % 2 + 1) * LANES)
        state_ref[band * modes : (band + 1) * modes, half] = high
        band += state_ref.shape[0] // (2 * modes)
        state_ref[band * modes : (band + 1) * modes, half] = low


def near_kernel(gated_ref, rate_ref, res_ref, near_ref):
    rows, width = gated_ref.shape
    per = LANES // GSIZE
    row = iota((rows, LANES), 0).astype(F32)
    group = iota((rows, LANES), 1) // GSIZE
    causal = iota((rows, LANES), 0) >= iota((rows, LANES), 1)
    for tile in range(width // LANES):
        cols = slice(tile * LANES, (tile + 1) * LANES)
        rate = rate_ref[:, cols]
        coeff = res_ref[:, cols] * jnp.exp(-rate * row)
        grow = jnp.exp(rate * row).T
        gated = gated_ref[:, cols]
        grow_high, grow_low = split(grow)
        coeff_high, coeff_low = split(coeff)
        zero = jnp.zeros_like(coeff_high)
        stack_high = jnp.concatenate([jnp.where(group == g, coeff_high, zero) for g in range(per)], 0)
        stack_low = jnp.concatenate([jnp.where(group == g, coeff_low, zero) for g in range(per)], 0)
        table = (
            jnp.dot(stack_high, grow_high, preferred_element_type=F32)
            + jnp.dot(stack_high, grow_low, preferred_element_type=F32)
            + jnp.dot(stack_low, grow_high, preferred_element_type=F32)
        )
        table = jnp.where(jnp.concatenate([causal] * per, 0), table, 0.0).astype(BF16)
        every = jnp.dot(table, gated, preferred_element_type=F32)
        near = jnp.zeros((rows, LANES), F32)
        for g in range(per):
            near = jnp.where(group == g, every[g * rows : (g + 1) * rows], near)
        near_ref[:, cols] = near


def fold(states, rate, exponent):
    high, low = states
    return jnp.exp(rate * exponent) * (high.astype(F32) + low.astype(F32))


def gather_states(where_ref, base, message, rate_ref, before, total):
    half = rate_ref.shape[0]
    states = (message[:half, :], message[half:, :])
    place, origin, ring = where_ref[base + 4], where_ref[base + 5], where_ref[base + 6]
    span = where_ref[base + 7].astype(F32)
    rate = -rate_ref[...] * span
    lag = jnp.maximum(place - 1 - origin, 0).astype(F32)
    here = jnp.where(origin < place, 1.0, 0.0)
    before = before + here * fold(states, rate, lag)
    total = total + fold(states, rate, (ring - 1 - origin).astype(F32))
    return before, total


def last_states_kernel(where_ref, message_ref, sums_ref, rate_ref, before_ref, total_ref):
    half = rate_ref.shape[0]
    before, total = gather_states(
        where_ref, 0, message_ref, rate_ref, sums_ref[:half, :], sums_ref[half:, :]
    )
    before_ref[...] = before
    total_ref[...] = total


def join_kernel(
    where_ref, first_ref, gated_ref, near_ref, before_ref, *refs
):
    *totals, band_ref, rate_ref, res_ref, gain_ref, out_ref, past_ref = refs
    rows, width = gated_ref.shape
    modes = GSIZE
    span = where_ref[7].astype(F32)
    band_rate = -band_ref[...] * span
    past_ref[...] = before_ref[...]
    for number, total in enumerate(totals):
        lag = (where_ref[4] + number * where_ref[6]).astype(F32)
        past_ref[...] += jnp.exp(band_rate * lag) * total[...]
    row = iota((rows, LANES), 0).astype(F32)
    same = iota((LANES, LANES), 0) // GSIZE == iota((LANES, LANES), 1) // GSIZE
    for tile in range(width // LANES):
        cols = slice(tile * LANES, (tile + 1) * LANES)
        coeff_high, coeff_low = split(res_ref[:, cols] * jnp.exp(-rate_ref[:, cols] * row))
        band, half = tile // 2, slice(tile % 2 * LANES, (tile % 2 + 1) * LANES)
        past = past_ref[band * modes : (band + 1) * modes, half]
        past = jnp.concatenate([past] * (LANES // GSIZE), 0)
        past_high, past_low = split(jnp.where(same, past, 0.0))
        far = (
            jnp.dot(coeff_high, past_high, preferred_element_type=F32)
            + jnp.dot(coeff_high, past_low, preferred_element_type=F32)
            + jnp.dot(coeff_low, past_high, preferred_element_type=F32)
        )
        direct = gain_ref[:, cols] * gated_ref[:, cols].astype(F32)
        out_ref[:, cols] = (first_ref[:, cols] * (far + near_ref[:, cols] + direct)).astype(BF16)


def attend_kernel(first, last, rows, blocks, scale, where_ref, q_ref, *refs):
    heads = q_ref.shape[0] // rows
    per = blocks + 4
    messages = where_ref.shape[0] // per
    kv_refs, refs = refs[:messages], refs[messages:]
    if first:
        rate_ref, acc_out, ml_out, sums_out = refs
    elif last:
        acc_in, ml_in, out_ref = refs
    else:
        rate_ref, acc_in, ml_in, sums_in, acc_out, ml_out, sums_out = refs
    chunk = 128
    count = blocks * rows
    if not last:
        half = rate_ref.shape[0]
        zero = jnp.zeros(rate_ref.shape, F32)
        sums = (zero, zero) if first else (sums_in[:half, :], sums_in[half:, :])
        for number, kv_ref in enumerate(kv_refs):
            sums = gather_states(where_ref, number * per, kv_ref[count:, :], rate_ref, *sums)
        sums_out[:half, :], sums_out[half:, :] = sums
    keys = jnp.concatenate([kv_ref[:count, :LANES] for kv_ref in kv_refs], 0)
    values = jnp.concatenate([kv_ref[:count, LANES:] for kv_ref in kv_refs], 0)
    values = jnp.concatenate([values, jnp.ones_like(values)], 1)
    lane_block = iota((1, messages * count), 1) // rows
    bias = jnp.zeros((1, messages * count), F32)
    for number in range(messages):
        for b in range(1 if first else 0, blocks):
            hidden = where_ref[number * per + b] == 0
            bias = bias + jnp.where((lane_block == number * blocks + b) & hidden, -1e30, 0.0)

    for number in range(q_ref.shape[0] // chunk):
        span = slice(number * chunk, (number + 1) * chunk)
        scores = lax.dot_general(
            q_ref[span, :], keys, (((1,), (1,)), ((), ())), preferred_element_type=F32
        )
        scores = scores * scale + bias
        if first:
            target = (number * chunk + iota(scores.shape, 0)) // heads
            source = iota(scores.shape, 1)
            scores = jnp.where((source > target) & (source < rows), -1e30, scores)
        largest = jnp.max(scores, axis=1, keepdims=True)
        if not first:
            before = ml_in[span, :1]
            largest = jnp.maximum(largest, before)
        weights = jnp.exp2(scores - largest).astype(BF16)
        mixed = jnp.dot(weights, values, preferred_element_type=F32)
        total = mixed[:, LANES : 2 * LANES]
        mixed = mixed[:, :LANES]
        if not first:
            shrink = jnp.exp2(before - largest)
            mixed = mixed + acc_in[span, :] * shrink
            total = total + ml_in[span, LANES - 1 :] * shrink
        if last:
            out_ref[span, :] = (mixed / total).astype(BF16)
        else:
            acc_out[span, :] = mixed
            lane = iota((chunk, LANES), 1)
            ml_out[span, :] = jnp.where(lane < LANES // 2, largest, total)


def body(streams, short_taps, modal_residue, modal_rate, skip_gain, queries, keys, values):
    rows, kinds, width = streams.shape
    taps = short_taps.shape[0]
    modes, groups = modal_rate.shape
    heads, size = queries.shape[1:]
    layers, ring = lax.axis_size("zh"), lax.axis_size("y")
    layer, place = lax.axis_index("zh"), lax.axis_index("y")
    devices = layers * ring

    kv = jnp.concatenate([keys[:, 0], values[:, 0]], axis=1)
    held = [kv] + [
        lax.ppermute(kv, "zh", [(z, z + s) for z in range(layers - s)]) for s in range(1, layers)
    ]

    by_kind = jnp.transpose(streams, (1, 0, 2))
    rim = lax.ppermute(by_kind[:, rows - 8 :], ("zh", "y"), [(i, i + 1) for i in range(devices - 1)])
    taps_full = jnp.repeat(short_taps.reshape(taps * kinds, groups), GSIZE, axis=1)
    bands = width // (2 * LANES)
    band_rate = modal_rate.reshape(modes, bands, groups // bands).transpose(1, 0, 2)
    band_rate = jnp.repeat(band_rate.reshape(bands * modes, groups // bands), GSIZE, axis=1)
    rate_row = modal_rate.T.reshape(1, groups * modes)
    res_row = modal_residue.T.reshape(1, groups * modes)
    wide = jax.ShapeDtypeStruct((rows, width), F32)
    first, gated, state = call(
        filter_kernel,
        [wide, jax.ShapeDtypeStruct((rows, width), BF16), jax.ShapeDtypeStruct((6 * modes, 2 * LANES), BF16)],
        vmem(4),
        4_000_000_000,
        4_000_000,
        [pltpu.VMEM((3, rows + 8, LANES), F32)],
    )(by_kind, rim, taps_full, rate_row)

    rows_q = queries.reshape(rows * heads, size)
    scale = LOG2E / math.sqrt(size)
    state_shape = [jax.ShapeDtypeStruct((rows * heads, LANES), F32)] * 2
    sums_shape = jax.ShapeDtypeStruct((2 * bands * modes, 2 * LANES), F32)
    band_shape = jax.ShapeDtypeStruct((bands * modes, 2 * LANES), F32)
    layer_seen = (layer >= jnp.arange(1, layers)).astype(jnp.int32)

    def describe(offset):
        origin = (place + offset) % ring
        return jnp.concatenate(
            [
                (origin < place)[None].astype(jnp.int32),
                layer_seen,
                jnp.stack([place, origin, jnp.int32(ring), jnp.int32(rows)]),
            ]
        )

    def attend(messages, offsets, carry, first=False, last=False):
        where = jnp.concatenate([describe(offset) for offset in offsets])
        return call(
            functools.partial(attend_kernel, first, last, rows, layers, scale),
            jax.ShapeDtypeStruct((rows * heads, size), BF16) if last else state_shape + [sums_shape],
            [smem()] + vmem(1 + len(messages) + len(carry)),
            1_000_000_000 * len(messages),
            3_000_000,
        )(where, rows_q, *messages, *carry)

    def turn(message, by):
        return lax.ppermute(message, "y", [(y, (y + by) % ring) for y in range(ring)])

    message = jnp.concatenate(held + [state], axis=0)
    pending, offsets, carry = [message], [0], (band_rate,)
    for step in range(1, ring // 2 + 1):
        both = 2 * step < ring
        sent = [turn(pending[0], 1)] + ([turn(pending[-1], -1)] if both else [])
        carry = attend(pending, offsets, carry, first=step == 1)
        if step == 1:
            near = call(near_kernel, wide, vmem(3), 4_000_000_000, 4_000_000)(
                gated, rate_row, res_row
            )
            *sent, near = lax.optimization_barrier((*sent, near))
        *sent, acc, highest, sums = lax.optimization_barrier((*sent, *carry))
        carry = (band_rate, acc, highest, sums)
        pending, offsets = sent, ([-step, step] if both else [-step])
    where = describe(offsets[0])
    before, total = call(
        last_states_kernel, [band_shape] * 2, [smem()] + vmem(3), 1_000_000, 500_000
    )(where, pending[0][layers * rows :], sums, band_rate)
    attn_out = attend(pending, offsets, (acc, highest), last=True).reshape(rows, heads, size)

    totals = [
        lax.ppermute(total, "zh", [(z, z + s) for z in range(layers - s)]) for s in range(1, layers)
    ]
    hyena_out = call(
        join_kernel,
        jax.ShapeDtypeStruct((rows, width), BF16),
        [smem()] + vmem(8 + len(totals)),
        500_000_000,
        2_000_000,
        [pltpu.VMEM((bands * modes, 2 * LANES), F32)],
    )(where, first, gated, near, before, *totals, band_rate, rate_row, res_row, skip_gain.reshape(1, width))
    return hyena_out, attn_out


def solution(mesh):
    names = ("dp", "zh", "y", "mp")
    dp, ctx, mp = (mesh.shape[name] for name in ("dp", "ctx", "mp"))
    ring = 8 if ctx % 8 == 0 else ctx
    finer = Mesh(mesh.devices.reshape(dp, ctx // ring, ring, mp), names)
    pos = ("dp", "zh", "y")
    in_specs = (
        P(pos, None, "mp"),
        P(None, None, "mp"),
        P(None, "mp"),
        P(None, "mp"),
        P("mp"),
        P(pos, "mp", None),
        P(pos, "mp", None),
        P(pos, "mp", None),
    )
    out_specs = (P(pos, "mp"), P(pos, "mp", None))
    return jax.shard_map(body, mesh=finer, in_specs=in_specs, out_specs=out_specs, check_vma=False)
```

```python
import functools
import math

import jax
import jax.numpy as jnp
from jax import lax
from jax.experimental import pallas as pl
from jax.experimental.pallas import tpu as pltpu
from jax.sharding import Mesh, PartitionSpec as P

GSIZE = 16
LANES = 128
LOG2E = 1.4426950408889634
HIGHEST = lax.Precision.HIGHEST
F32 = jnp.float32
BF16 = jnp.bfloat16


def vmem(count):
    return [pl.BlockSpec(memory_space=pltpu.VMEM)] * count


def smem():
    return pl.BlockSpec(memory_space=pltpu.SMEM)


def call(kernel, out_shape, in_specs, flops, moved, scratch=()):
    many = isinstance(out_shape, (list, tuple))
    return pl.pallas_call(
        kernel,
        out_shape=out_shape,
        in_specs=in_specs,
        out_specs=vmem(len(out_shape)) if many else vmem(1)[0],
        scratch_shapes=list(scratch),
        compiler_params=pltpu.CompilerParams(vmem_limit_bytes=16 * 1024 * 1024),
        cost_estimate=pl.CostEstimate(flops=flops, bytes_accessed=moved, transcendentals=0),
    )


def iota(shape, dim):
    return lax.broadcasted_iota(jnp.int32, shape, dim)


def split(value):
    high = value.astype(BF16)
    return high, (value - high.astype(F32)).astype(BF16)


def filter_kernel(st_ref, rim_ref, taps_ref, rate_ref, first_ref, gated_ref, state_ref, ext):
    rows, width = gated_ref.shape
    pad = rim_ref.shape[1]
    taps = taps_ref.shape[0] // 3
    modes = LANES // (LANES // GSIZE)
    row = iota((rows, LANES), 0).astype(F32)
    same = iota((LANES, LANES), 0) // GSIZE == iota((LANES, LANES), 1) // GSIZE
    for tile in range(width // LANES):
        cols = slice(tile * LANES, (tile + 1) * LANES)
        for j in range(3):
            ext[j, :pad, :] = rim_ref[j, :, cols].astype(F32)
            ext[j, pad:, :] = st_ref[j, :, cols].astype(F32)
        filtered = []
        for j in range(3):
            total = taps_ref[j : j + 1, cols] * ext[j, pad : pad + rows, :]
            for k in range(1, taps):
                tap = taps_ref[3 * k + j : 3 * k + j + 1, cols]
                total = total + tap * ext[j, pad - k : pad - k + rows, :]
            filtered.append(total)
        first_ref[:, cols] = filtered[0]
        gated = (filtered[1] * filtered[2]).astype(BF16)
        gated_ref[:, cols] = gated
        decay = jnp.exp(-rate_ref[:, cols] * (float(rows) - row)).T
        high, low = split(decay)
        full = jnp.dot(high, gated, preferred_element_type=F32) + jnp.dot(
            low, gated, preferred_element_type=F32
        )
        full = jnp.where(same, full, 0.0)
        state = full[:modes]
        for g in range(1, LANES // GSIZE):
            state = state + full[g * modes : (g + 1) * modes]
        high, low = split(state)
        band, half = tile // 2, slice(tile % 2 * LANES, (tile % 2 + 1) * LANES)
        state_ref[band * modes : (band + 1) * modes, half] = high
        band += state_ref.shape[0] // (2 * modes)
        state_ref[band * modes : (band + 1) * modes, half] = low


def near_kernel(gated_ref, rate_ref, res_ref, near_ref):
    rows, width = gated_ref.shape
    per = LANES // GSIZE
    row = iota((rows, LANES), 0).astype(F32)
    group = iota((rows, LANES), 1) // GSIZE
    causal = iota((rows, LANES), 0) >= iota((rows, LANES), 1)
    for tile in range(width // LANES):
        cols = slice(tile * LANES, (tile + 1) * LANES)
        rate = rate_ref[:, cols]
        coeff = res_ref[:, cols] * jnp.exp(-rate * row)
        grow = jnp.exp(rate * row).T
        gated = gated_ref[:, cols]
        grow_high, grow_low = split(grow)
        coeff_high, coeff_low = split(coeff)
        zero = jnp.zeros_like(coeff_high)
        stack_high = jnp.concatenate([jnp.where(group == g, coeff_high, zero) for g in range(per)], 0)
        stack_low = jnp.concatenate([jnp.where(group == g, coeff_low, zero) for g in range(per)], 0)
        table = (
            jnp.dot(stack_high, grow_high, preferred_element_type=F32)
            + jnp.dot(stack_high, grow_low, preferred_element_type=F32)
            + jnp.dot(stack_low, grow_high, preferred_element_type=F32)
        )
        table = jnp.where(jnp.concatenate([causal] * per, 0), table, 0.0).astype(BF16)
        every = jnp.dot(table, gated, preferred_element_type=F32)
        near = jnp.zeros((rows, LANES), F32)
        for g in range(per):
            near = jnp.where(group == g, every[g * rows : (g + 1) * rows], near)
        near_ref[:, cols] = near


def fold(states, rate, exponent):
    high, low = states
    return jnp.exp(rate * exponent) * (high.astype(F32) + low.astype(F32))


def gather_states(where_ref, base, message, rate_ref, before, total):
    half = rate_ref.shape[0]
    states = (message[:half, :], message[half:, :])
    place, origin, ring = where_ref[base + 4], where_ref[base + 5], where_ref[base + 6]
    span = where_ref[base + 7].astype(F32)
    rate = -rate_ref[...] * span
    lag = jnp.maximum(place - 1 - origin, 0).astype(F32)
    here = jnp.where(origin < place, 1.0, 0.0)
    before = before + here * fold(states, rate, lag)
    total = total + fold(states, rate, (ring - 1 - origin).astype(F32))
    return before, total


def last_states_kernel(where_ref, message_ref, sums_ref, rate_ref, before_ref, total_ref):
    half = rate_ref.shape[0]
    before, total = gather_states(
        where_ref, 0, message_ref, rate_ref, sums_ref[:half, :], sums_ref[half:, :]
    )
    before_ref[...] = before
    total_ref[...] = total


def join_kernel(
    where_ref, first_ref, gated_ref, near_ref, before_ref, *refs
):
    *totals, band_ref, rate_ref, res_ref, gain_ref, out_ref, past_ref = refs
    rows, width = gated_ref.shape
    modes = GSIZE
    span = where_ref[7].astype(F32)
    band_rate = -band_ref[...] * span
    past_ref[...] = before_ref[...]
    for number, total in enumerate(totals):
        lag = (where_ref[4] + number * where_ref[6]).astype(F32)
        past_ref[...] += jnp.exp(band_rate * lag) * total[...]
    row = iota((rows, LANES), 0).astype(F32)
    same = iota((LANES, LANES), 0) // GSIZE == iota((LANES, LANES), 1) // GSIZE
    for tile in range(width // LANES):
        cols = slice(tile * LANES, (tile + 1) * LANES)
        coeff_high, coeff_low = split(res_ref[:, cols] * jnp.exp(-rate_ref[:, cols] * row))
        band, half = tile // 2, slice(tile % 2 * LANES, (tile % 2 + 1) * LANES)
        past = past_ref[band * modes : (band + 1) * modes, half]
        past = jnp.concatenate([past] * (LANES // GSIZE), 0)
        past_high, past_low = split(jnp.where(same, past, 0.0))
        far = (
            jnp.dot(coeff_high, past_high, preferred_element_type=F32)
            + jnp.dot(coeff_high, past_low, preferred_element_type=F32)
            + jnp.dot(coeff_low, past_high, preferred_element_type=F32)
        )
        direct = gain_ref[:, cols] * gated_ref[:, cols].astype(F32)
        out_ref[:, cols] = (first_ref[:, cols] * (far + near_ref[:, cols] + direct)).astype(BF16)


def attend_kernel(first, last, rows, blocks, scale, where_ref, q_ref, *refs):
    heads = q_ref.shape[0] // rows
    per = blocks + 4
    messages = where_ref.shape[0] // per
    kv_refs, refs = refs[:messages], refs[messages:]
    if first:
        rate_ref, acc_out, ml_out, sums_out = refs
    elif last:
        acc_in, ml_in, out_ref = refs
    else:
        rate_ref, acc_in, ml_in, sums_in, acc_out, ml_out, sums_out = refs
    chunk = 128
    count = blocks * rows
    if not last:
        half = rate_ref.shape[0]
        zero = jnp.zeros(rate_ref.shape, F32)
        sums = (zero, zero) if first else (sums_in[:half, :], sums_in[half:, :])
        for number, kv_ref in enumerate(kv_refs):
            sums = gather_states(where_ref, number * per, kv_ref[count:, :], rate_ref, *sums)
        sums_out[:half, :], sums_out[half:, :] = sums
    keys = jnp.concatenate([kv_ref[:count, :LANES] for kv_ref in kv_refs], 0)
    values = jnp.concatenate([kv_ref[:count, LANES:] for kv_ref in kv_refs], 0)
    values = jnp.concatenate([values, jnp.ones_like(values)], 1)
    lane_block = iota((1, messages * count), 1) // rows
    bias = jnp.zeros((1, messages * count), F32)
    for number in range(messages):
        for b in range(1 if first else 0, blocks):
            hidden = where_ref[number * per + b] == 0
            bias = bias + jnp.where((lane_block == number * blocks + b) & hidden, -1e30, 0.0)

    for number in range(q_ref.shape[0] // chunk):
        span = slice(number * chunk, (number + 1) * chunk)
        scores = lax.dot_general(
            q_ref[span, :], keys, (((1,), (1,)), ((), ())), preferred_element_type=F32
        )
        scores = scores * scale + bias
        if first:
            target = (number * chunk + iota(scores.shape, 0)) // heads
            source = iota(scores.shape, 1)
            scores = jnp.where((source > target) & (source < rows), -1e30, scores)
        largest = jnp.max(scores, axis=1, keepdims=True)
        if not first:
            before = ml_in[span, :1]
            largest = jnp.maximum(largest, before)
        weights = jnp.exp2(scores - largest).astype(BF16)
        mixed = jnp.dot(weights, values, preferred_element_type=F32)
        total = mixed[:, LANES : 2 * LANES]
        mixed = mixed[:, :LANES]
        if not first:
            shrink = jnp.exp2(before - largest)
            mixed = mixed + acc_in[span, :] * shrink
            total = total + ml_in[span, LANES - 1 :] * shrink
        if last:
            out_ref[span, :] = (mixed / total).astype(BF16)
        else:
            acc_out[span, :] = mixed
            lane = iota((chunk, LANES), 1)
            ml_out[span, :] = jnp.where(lane < LANES // 2, largest, total)


def body(streams, short_taps, modal_residue, modal_rate, skip_gain, queries, keys, values):
    rows, kinds, width = streams.shape
    taps = short_taps.shape[0]
    modes, groups = modal_rate.shape
    heads, size = queries.shape[1:]
    layers, ring = lax.axis_size("zh"), lax.axis_size("y")
    layer, place = lax.axis_index("zh"), lax.axis_index("y")
    devices = layers * ring

    kv = jnp.concatenate([keys[:, 0], values[:, 0]], axis=1)
    held = [kv] + [
        lax.ppermute(kv, "zh", [(z, z + s) for z in range(layers - s)]) for s in range(1, layers)
    ]

    by_kind = jnp.transpose(streams, (1, 0, 2))
    rim = lax.ppermute(by_kind[:, rows - 8 :], ("zh", "y"), [(i, i + 1) for i in range(devices - 1)])
    taps_full = jnp.repeat(short_taps.reshape(taps * kinds, groups), GSIZE, axis=1)
    bands = width // (2 * LANES)
    band_rate = modal_rate.reshape(modes, bands, groups // bands).transpose(1, 0, 2)
    band_rate = jnp.repeat(band_rate.reshape(bands * modes, groups // bands), GSIZE, axis=1)
    rate_row = modal_rate.T.reshape(1, groups * modes)
    res_row = modal_residue.T.reshape(1, groups * modes)
    wide = jax.ShapeDtypeStruct((rows, width), F32)
    first, gated, state = call(
        filter_kernel,
        [wide, jax.ShapeDtypeStruct((rows, width), BF16), jax.ShapeDtypeStruct((6 * modes, 2 * LANES), BF16)],
        vmem(4),
        4_000_000_000,
        4_000_000,
        [pltpu.VMEM((3, rows + 8, LANES), F32)],
    )(by_kind, rim, taps_full, rate_row)

    rows_q = queries.reshape(rows * heads, size)
    scale = LOG2E / math.sqrt(size)
    state_shape = [jax.ShapeDtypeStruct((rows * heads, LANES), F32)] * 2
    sums_shape = jax.ShapeDtypeStruct((2 * bands * modes, 2 * LANES), F32)
    band_shape = jax.ShapeDtypeStruct((bands * modes, 2 * LANES), F32)
    layer_seen = (layer >= jnp.arange(1, layers)).astype(jnp.int32)

    def describe(offset):
        origin = (place + offset) % ring
        return jnp.concatenate(
            [
                (origin < place)[None].astype(jnp.int32),
                layer_seen,
                jnp.stack([place, origin, jnp.int32(ring), jnp.int32(rows)]),
            ]
        )

    def attend(messages, offsets, carry, first=False, last=False):
        where = jnp.concatenate([describe(offset) for offset in offsets])
        return call(
            functools.partial(attend_kernel, first, last, rows, layers, scale),
            jax.ShapeDtypeStruct((rows * heads, size), BF16) if last else state_shape + [sums_shape],
            [smem()] + vmem(1 + len(messages) + len(carry)),
            1_000_000_000 * len(messages),
            3_000_000,
        )(where, rows_q, *messages, *carry)

    def turn(message, by):
        return lax.ppermute(message, "y", [(y, (y + by) % ring) for y in range(ring)])

    message = jnp.concatenate(held + [state], axis=0)
    pending, offsets, carry = [message], [0], (band_rate,)
    for step in range(1, ring // 2 + 1):
        both = 2 * step < ring
        sent = [turn(pending[0], 1)] + ([turn(pending[-1], -1)] if both else [])
        carry = attend(pending, offsets, carry, first=step == 1)
        acc, highest, sums = carry
        *sent, sums = lax.optimization_barrier((*sent, sums))
        carry = (band_rate, acc, highest, sums)
        pending, offsets = sent, ([-step, step] if both else [-step])
    where = describe(offsets[0])
    before, total = call(
        last_states_kernel, [band_shape] * 2, [smem()] + vmem(3), 1_000_000, 500_000
    )(where, pending[0][layers * rows :], sums, band_rate)
    late, _ = lax.optimization_barrier((gated, total))
    near = call(near_kernel, wide, vmem(3), 4_000_000_000, 4_000_000)(late, rate_row, res_row)
    attn_out = attend(pending, offsets, (acc, highest), last=True).reshape(rows, heads, size)

    totals = [
        lax.ppermute(total, "zh", [(z, z + s) for z in range(layers - s)]) for s in range(1, layers)
    ]
    hyena_out = call(
        join_kernel,
        jax.ShapeDtypeStruct((rows, width), BF16),
        [smem()] + vmem(8 + len(totals)),
        500_000_000,
        2_000_000,
        [pltpu.VMEM((bands * modes, 2 * LANES), F32)],
    )(where, first, gated, near, before, *totals, band_rate, rate_row, res_row, skip_gain.reshape(1, width))
    return hyena_out, attn_out


def solution(mesh):
    names = ("dp", "zh", "y", "mp")
    dp, ctx, mp = (mesh.shape[name] for name in ("dp", "ctx", "mp"))
    ring = 8 if ctx % 8 == 0 else ctx
    finer = Mesh(mesh.devices.reshape(dp, ctx // ring, ring, mp), names)
    pos = ("dp", "zh", "y")
    in_specs = (
        P(pos, None, "mp"),
        P(None, None, "mp"),
        P(None, "mp"),
        P(None, "mp"),
        P("mp"),
        P(pos, "mp", None),
        P(pos, "mp", None),
        P(pos, "mp", None),
    )
    out_specs = (P(pos, "mp"), P(pos, "mp", None))
    return jax.shard_map(body, mesh=finer, in_specs=in_specs, out_specs=out_specs, check_vma=False)
```

```python
import functools
import math

import jax
import jax.numpy as jnp
from jax import lax
from jax.experimental import pallas as pl
from jax.experimental.pallas import tpu as pltpu
from jax.sharding import Mesh, PartitionSpec as P

GSIZE = 16
LANES = 128
LOG2E = 1.4426950408889634
HIGHEST = lax.Precision.HIGHEST
F32 = jnp.float32
BF16 = jnp.bfloat16


def vmem(count):
    return [pl.BlockSpec(memory_space=pltpu.VMEM)] * count


def smem():
    return pl.BlockSpec(memory_space=pltpu.SMEM)


def call(kernel, out_shape, in_specs, flops, moved, scratch=()):
    many = isinstance(out_shape, (list, tuple))
    return pl.pallas_call(
        kernel,
        out_shape=out_shape,
        in_specs=in_specs,
        out_specs=vmem(len(out_shape)) if many else vmem(1)[0],
        scratch_shapes=list(scratch),
        compiler_params=pltpu.CompilerParams(vmem_limit_bytes=16 * 1024 * 1024),
        cost_estimate=pl.CostEstimate(flops=flops, bytes_accessed=moved, transcendentals=0),
    )


def iota(shape, dim):
    return lax.broadcasted_iota(jnp.int32, shape, dim)


def split(value):
    high = value.astype(BF16)
    return high, (value - high.astype(F32)).astype(BF16)


def filter_kernel(st_ref, rim_ref, taps_ref, rate_ref, first_ref, gated_ref, state_ref, ext):
    rows, width = gated_ref.shape
    pad = rim_ref.shape[1]
    taps = taps_ref.shape[0] // 3
    modes = LANES // (LANES // GSIZE)
    row = iota((rows, LANES), 0).astype(F32)
    same = iota((LANES, LANES), 0) // GSIZE == iota((LANES, LANES), 1) // GSIZE
    for tile in range(width // LANES):
        cols = slice(tile * LANES, (tile + 1) * LANES)
        for j in range(3):
            ext[j, :pad, :] = rim_ref[j, :, cols].astype(F32)
            ext[j, pad:, :] = st_ref[j, :, cols].astype(F32)
        filtered = []
        for j in range(3):
            total = taps_ref[j : j + 1, cols] * ext[j, pad : pad + rows, :]
            for k in range(1, taps):
                tap = taps_ref[3 * k + j : 3 * k + j + 1, cols]
                total = total + tap * ext[j, pad - k : pad - k + rows, :]
            filtered.append(total)
        first_ref[:, cols] = filtered[0]
        gated = (filtered[1] * filtered[2]).astype(BF16)
        gated_ref[:, cols] = gated
        decay = jnp.exp(-rate_ref[:, cols] * (float(rows) - row)).T
        high, low = split(decay)
        full = jnp.dot(high, gated, preferred_element_type=F32) + jnp.dot(
            low, gated, preferred_element_type=F32
        )
        full = jnp.where(same, full, 0.0)
        state = full[:modes]
        for g in range(1, LANES // GSIZE):
            state = state + full[g * modes : (g + 1) * modes]
        high, low = split(state)
        band, half = tile // 2, slice(tile % 2 * LANES, (tile % 2 + 1) * LANES)
        state_ref[band * modes : (band + 1) * modes, half] = high
        band += state_ref.shape[0] // (2 * modes)
        state_ref[band * modes : (band + 1) * modes, half] = low


def near_kernel(gated_ref, rate_ref, res_ref, near_ref):
    rows, width = gated_ref.shape
    per = LANES // GSIZE
    row = iota((rows, LANES), 0).astype(F32)
    group = iota((rows, LANES), 1) // GSIZE
    causal = iota((rows, LANES), 0) >= iota((rows, LANES), 1)
    for tile in range(width // LANES):
        cols = slice(tile * LANES, (tile + 1) * LANES)
        rate = rate_ref[:, cols]
        coeff = res_ref[:, cols] * jnp.exp(-rate * row)
        grow = jnp.exp(rate * row).T
        gated = gated_ref[:, cols]
        grow_high, grow_low = split(grow)
        coeff_high, coeff_low = split(coeff)
        zero = jnp.zeros_like(coeff_high)
        stack_high = jnp.concatenate([jnp.where(group == g, coeff_high, zero) for g in range(per)], 0)
        stack_low = jnp.concatenate([jnp.where(group == g, coeff_low, zero) for g in range(per)], 0)
        table = (
            jnp.dot(stack_high, grow_high, preferred_element_type=F32)
            + jnp.dot(stack_high, grow_low, preferred_element_type=F32)
            + jnp.dot(stack_low, grow_high, preferred_element_type=F32)
        )
        table = jnp.where(jnp.concatenate([causal] * per, 0), table, 0.0).astype(BF16)
        every = jnp.dot(table, gated, preferred_element_type=F32)
        near = jnp.zeros((rows, LANES), F32)
        for g in range(per):
            near = jnp.where(group == g, every[g * rows : (g + 1) * rows], near)
        near_ref[:, cols] = near


def fold(states, rate, exponent):
    high, low = states
    return jnp.exp(rate * exponent) * (high.astype(F32) + low.astype(F32))


def gather_states(where_ref, base, message, rate_ref, before, total):
    half = rate_ref.shape[0]
    own = (message[:half, :], message[half : 2 * half, :])
    older = (message[2 * half : 3 * half, :], message[3 * half :, :])
    place, origin, ring = where_ref[base + 4], where_ref[base + 5], where_ref[base + 6]
    span = where_ref[base + 7].astype(F32)
    rate = -rate_ref[...] * span
    lag = jnp.maximum(place - 1 - origin, 0).astype(F32)
    here = jnp.where(origin < place, 1.0, 0.0)
    before = before + here * fold(own, rate, lag)
    total = total + fold(older, rate, (ring - 1 - origin).astype(F32))
    return before, total


def layers_kernel(where_ref, rate_ref, *refs):
    *states, out_ref = refs
    half = rate_ref.shape[0]
    rate = -rate_ref[...] * where_ref[7].astype(F32)
    total = jnp.zeros(rate_ref.shape, F32)
    for number, state in enumerate(states):
        pair = (state[:half, :], state[half:, :])
        total = total + fold(pair, rate, (number * where_ref[6]).astype(F32))
    high, low = split(total)
    out_ref[:half, :] = high
    out_ref[half:, :] = low


def last_states_kernel(where_ref, message_ref, sums_ref, rate_ref, before_ref, total_ref):
    half = rate_ref.shape[0]
    before, total = gather_states(
        where_ref, 0, message_ref, rate_ref, sums_ref[:half, :], sums_ref[half:, :]
    )
    before_ref[...] = before
    total_ref[...] = total


def join_kernel(
    where_ref, first_ref, gated_ref, near_ref, before_ref, *refs
):
    total_ref, band_ref, rate_ref, res_ref, gain_ref, out_ref, past_ref = refs
    rows, width = gated_ref.shape
    modes = GSIZE
    span = where_ref[7].astype(F32)
    band_rate = -band_ref[...] * span
    lag = where_ref[4].astype(F32)
    past_ref[...] = before_ref[...] + jnp.exp(band_rate * lag) * total_ref[...]
    row = iota((rows, LANES), 0).astype(F32)
    same = iota((LANES, LANES), 0) // GSIZE == iota((LANES, LANES), 1) // GSIZE
    for tile in range(width // LANES):
        cols = slice(tile * LANES, (tile + 1) * LANES)
        coeff_high, coeff_low = split(res_ref[:, cols] * jnp.exp(-rate_ref[:, cols] * row))
        band, half = tile // 2, slice(tile % 2 * LANES, (tile % 2 + 1) * LANES)
        past = past_ref[band * modes : (band + 1) * modes, half]
        past = jnp.concatenate([past] * (LANES // GSIZE), 0)
        past_high, past_low = split(jnp.where(same, past, 0.0))
        far = (
            jnp.dot(coeff_high, past_high, preferred_element_type=F32)
            + jnp.dot(coeff_high, past_low, preferred_element_type=F32)
            + jnp.dot(coeff_low, past_high, preferred_element_type=F32)
        )
        direct = gain_ref[:, cols] * gated_ref[:, cols].astype(F32)
        out_ref[:, cols] = (first_ref[:, cols] * (far + near_ref[:, cols] + direct)).astype(BF16)


def attend_kernel(first, last, rows, blocks, scale, where_ref, q_ref, *refs):
    heads = q_ref.shape[0] // rows
    per = blocks + 4
    messages = where_ref.shape[0] // per
    kv_refs, refs = refs[:messages], refs[messages:]
    if first:
        rate_ref, acc_out, ml_out, sums_out = refs
    elif last:
        acc_in, ml_in, out_ref = refs
    else:
        rate_ref, acc_in, ml_in, sums_in, acc_out, ml_out, sums_out = refs
    chunk = 128
    count = blocks * rows
    if not last:
        half = rate_ref.shape[0]
        zero = jnp.zeros(rate_ref.shape, F32)
        sums = (zero, zero) if first else (sums_in[:half, :], sums_in[half:, :])
        for number, kv_ref in enumerate(kv_refs):
            sums = gather_states(where_ref, number * per, kv_ref[count:, :], rate_ref, *sums)
        sums_out[:half, :], sums_out[half:, :] = sums
    keys = jnp.concatenate([kv_ref[:count, :LANES] for kv_ref in kv_refs], 0)
    values = jnp.concatenate([kv_ref[:count, LANES:] for kv_ref in kv_refs], 0)
    values = jnp.concatenate([values, jnp.ones_like(values)], 1)
    lane_block = iota((1, messages * count), 1) // rows
    bias = jnp.zeros((1, messages * count), F32)
    for number in range(messages):
        for b in range(1 if first else 0, blocks):
            hidden = where_ref[number * per + b] == 0
            bias = bias + jnp.where((lane_block == number * blocks + b) & hidden, -1e30, 0.0)

    for number in range(q_ref.shape[0] // chunk):
        span = slice(number * chunk, (number + 1) * chunk)
        scores = lax.dot_general(
            q_ref[span, :], keys, (((1,), (1,)), ((), ())), preferred_element_type=F32
        )
        scores = scores * scale + bias
        if first:
            target = (number * chunk + iota(scores.shape, 0)) // heads
            source = iota(scores.shape, 1)
            scores = jnp.where((source > target) & (source < rows), -1e30, scores)
        largest = jnp.max(scores, axis=1, keepdims=True)
        if not first:
            before = ml_in[span, :1]
            largest = jnp.maximum(largest, before)
        weights = jnp.exp2(scores - largest).astype(BF16)
        mixed = jnp.dot(weights, values, preferred_element_type=F32)
        total = mixed[:, LANES : 2 * LANES]
        mixed = mixed[:, :LANES]
        if not first:
            shrink = jnp.exp2(before - largest)
            mixed = mixed + acc_in[span, :] * shrink
            total = total + ml_in[span, LANES - 1 :] * shrink
        if last:
            out_ref[span, :] = (mixed / total).astype(BF16)
        else:
            acc_out[span, :] = mixed
            lane = iota((chunk, LANES), 1)
            ml_out[span, :] = jnp.where(lane < LANES // 2, largest, total)


def body(streams, short_taps, modal_residue, modal_rate, skip_gain, queries, keys, values):
    rows, kinds, width = streams.shape
    taps = short_taps.shape[0]
    modes, groups = modal_rate.shape
    heads, size = queries.shape[1:]
    layers, ring = lax.axis_size("zh"), lax.axis_size("y")
    layer, place = lax.axis_index("zh"), lax.axis_index("y")
    devices = layers * ring

    kv = jnp.concatenate([keys[:, 0], values[:, 0]], axis=1)
    held = [kv] + [
        lax.ppermute(kv, "zh", [(z, z + s) for z in range(layers - s)]) for s in range(1, layers)
    ]

    by_kind = jnp.transpose(streams, (1, 0, 2))
    rim = lax.ppermute(by_kind[:, rows - 8 :], ("zh", "y"), [(i, i + 1) for i in range(devices - 1)])
    taps_full = jnp.repeat(short_taps.reshape(taps * kinds, groups), GSIZE, axis=1)
    bands = width // (2 * LANES)
    band_rate = modal_rate.reshape(modes, bands, groups // bands).transpose(1, 0, 2)
    band_rate = jnp.repeat(band_rate.reshape(bands * modes, groups // bands), GSIZE, axis=1)
    rate_row = modal_rate.T.reshape(1, groups * modes)
    res_row = modal_residue.T.reshape(1, groups * modes)
    wide = jax.ShapeDtypeStruct((rows, width), F32)
    first, gated, state = call(
        filter_kernel,
        [wide, jax.ShapeDtypeStruct((rows, width), BF16), jax.ShapeDtypeStruct((6 * modes, 2 * LANES), BF16)],
        vmem(4),
        4_000_000_000,
        4_000_000,
        [pltpu.VMEM((3, rows + 8, LANES), F32)],
    )(by_kind, rim, taps_full, rate_row)

    rows_q = queries.reshape(rows * heads, size)
    scale = LOG2E / math.sqrt(size)
    state_shape = [jax.ShapeDtypeStruct((rows * heads, LANES), F32)] * 2
    sums_shape = jax.ShapeDtypeStruct((2 * bands * modes, 2 * LANES), F32)
    band_shape = jax.ShapeDtypeStruct((bands * modes, 2 * LANES), F32)
    layer_seen = (layer >= jnp.arange(1, layers)).astype(jnp.int32)

    def describe(offset):
        origin = (place + offset) % ring
        return jnp.concatenate(
            [
                (origin < place)[None].astype(jnp.int32),
                layer_seen,
                jnp.stack([place, origin, jnp.int32(ring), jnp.int32(rows)]),
            ]
        )

    def attend(messages, offsets, carry, first=False, last=False):
        where = jnp.concatenate([describe(offset) for offset in offsets])
        return call(
            functools.partial(attend_kernel, first, last, rows, layers, scale),
            jax.ShapeDtypeStruct((rows * heads, size), BF16) if last else state_shape + [sums_shape],
            [smem()] + vmem(1 + len(messages) + len(carry)),
            1_000_000_000 * len(messages),
            3_000_000,
        )(where, rows_q, *messages, *carry)

    def turn(message, by):
        return lax.ppermute(message, "y", [(y, (y + by) % ring) for y in range(ring)])

    states = [
        lax.ppermute(state, "zh", [(z, z + s) for z in range(layers - s)]) for s in range(1, layers)
    ]
    near = call(near_kernel, wide, vmem(3), 4_000_000_000, 4_000_000)(gated, rate_row, res_row)
    *states, near = lax.optimization_barrier((*states, near))
    older = call(
        layers_kernel, jax.ShapeDtypeStruct(state.shape, BF16), [smem()] + vmem(layers), 1_000_000, 500_000
    )(describe(0), band_rate, *states)
    message = jnp.concatenate(held + [state, older], axis=0)
    pending, offsets, carry = [message], [0], (band_rate,)
    for step in range(1, ring // 2 + 1):
        both = 2 * step < ring
        sent = [turn(pending[0], 1)] + ([turn(pending[-1], -1)] if both else [])
        carry = attend(pending, offsets, carry, first=step == 1)
        acc, highest, sums = carry
        *sent, sums = lax.optimization_barrier((*sent, sums))
        carry = (band_rate, acc, highest, sums)
        pending, offsets = sent, ([-step, step] if both else [-step])
    where = describe(offsets[0])
    before, total = call(
        last_states_kernel, [band_shape] * 2, [smem()] + vmem(3), 1_000_000, 500_000
    )(where, pending[0][layers * rows :], sums, band_rate)
    attn_out = attend(pending, offsets, (acc, highest), last=True).reshape(rows, heads, size)

    hyena_out = call(
        join_kernel,
        jax.ShapeDtypeStruct((rows, width), BF16),
        [smem()] + vmem(9),
        500_000_000,
        2_000_000,
        [pltpu.VMEM((bands * modes, 2 * LANES), F32)],
    )(where, first, gated, near, before, total, band_rate, rate_row, res_row, skip_gain.reshape(1, width))
    return hyena_out, attn_out


def solution(mesh):
    names = ("dp", "zh", "y", "mp")
    dp, ctx, mp = (mesh.shape[name] for name in ("dp", "ctx", "mp"))
    ring = 8 if ctx % 8 == 0 else ctx
    finer = Mesh(mesh.devices.reshape(dp, ctx // ring, ring, mp), names)
    pos = ("dp", "zh", "y")
    in_specs = (
        P(pos, None, "mp"),
        P(None, None, "mp"),
        P(None, "mp"),
        P(None, "mp"),
        P("mp"),
        P(pos, "mp", None),
        P(pos, "mp", None),
        P(pos, "mp", None),
    )
    out_specs = (P(pos, "mp"), P(pos, "mp", None))
    return jax.shard_map(body, mesh=finer, in_specs=in_specs, out_specs=out_specs, check_vma=False)
```
